32 devices in a mesh: inst: 16 (over z, y, core), tp: 2 (over x).
Axes of the slice: x: 2, y: 2, z: 4, core: 2. Of those that a mesh axis runs over, the one named last changes fastest.
Arguments:
- hidden_state: bfloat16 [2048, 6144], P('inst', 'tp'), may hold values from -3000 to 3000
- norm_gain: bfloat16 [6144], P('tp'), may hold values from 0.099609375 to 1.8984375
- kv_weight: bfloat16 [6144, 8, 256], P('tp'), may hold values from -0.078125 to 0.078125
- queries: bfloat16 [2048, 48, 128], P('inst', 'tp'), may hold values from -120 to 120
- pool_keys: bfloat16 [320, 8, 128, 128], P('inst', 'tp'), may hold values from -6 to 6
- pool_values: bfloat16 [320, 8, 128, 128], P('inst', 'tp'), may hold values from -6 to 6
- page_table: int32 [2048, 12], P('inst'), may hold values from 0 to 19, as said below
- lengths: int32 [2048], P('inst'), may hold values from 2 to 1536
- move_target: int32 [128, 1], P('inst'), may hold values from 0 to 15; in each aligned block of 8 rows (0 to 7, 8 to 15, ...) no two rows name the same one
- move_page: int32 [128], P('inst'), may hold values from 0 to 19
- move_request: int32 [128], P('inst'), may hold values from 0 to 127
Outputs:
- attention_out: bfloat16 [2048, 6144], P('inst', 'tp')
- new_kv: bfloat16 [2048, 8, 256], P('inst', 'tp')
The draws below stay inside these ranges and needn't reach their ends.
Inputs may be any that keep to these rules, and one draw needn't show every extreme that they name: `page_table`: each row names 12 distinct pages of its instance's pool. `move_target`: the 8 rows of one instance never name the same destination twice.
All inputs are finite; a program needn't handle non-finite values.
Results may differ from the reference program's by a relative error of at most 0.005.
Values may be sent and summed in bfloat16 or wider, within the bound.
A program may use at most 128 MiB of HBM per device.

```python
import math
import jax
import jax.numpy as jnp
import numpy as np
from jax import lax

D = 6144
QH = 48
KVH = 8
HD = 128
PAGE = 128
MAXP = 12
POOL = 20
REQ = 128
MIG = 8
MIGS = 128
ROWS = 2048
PAGES = 320
N_INST = 16


def keys_base(key):
    sample = jax.random.normal(jax.random.fold_in(key, 500), (PAGES, KVH, PAGE, HD), jnp.float32)
    return jnp.clip(sample, -6.0, 6.0)


def table_base(key):
    rank_keys = jax.random.randint(jax.random.fold_in(key, 600), (ROWS, POOL), 0, 1048576)
    rank_keys = rank_keys * POOL + jnp.arange(POOL, dtype=jnp.int32)[None, :]
    ordering = jnp.argsort(rank_keys, axis=1)
    return ordering[:, :MAXP].astype(jnp.int32)


def draw_page_table(key, part):
    shared = table_base(key)
    return shared


def draw_pool_keys(key, part):
    shared = keys_base(key)
    return shared.astype(jnp.bfloat16)


def draw_queries(key, part):
    key = jax.random.fold_in(key, 7)
    values = jnp.clip(2.5 * jax.random.normal(key, (ROWS, QH, HD), jnp.float32), -15.0, 15.0)
    return values.astype(jnp.bfloat16)


def draw_hidden_state(key, part):
    key = jax.random.fold_in(key, 11)
    draw_one = jax.random.fold_in(key, 1)
    draw_two = jax.random.fold_in(key, 2)
    draw_three = jax.random.fold_in(key, 3)
    rising = 3.0 ** (jnp.arange(D, dtype=jnp.float32) / (D - 1))
    base_draw = jnp.clip(jax.random.normal(draw_one, (ROWS, D), jnp.float32), -6.0, 6.0)
    row_scale = jnp.power(10.0, jax.random.uniform(draw_two, (ROWS, 1), jnp.float32, 0.0, 1.0))
    col_scale = jnp.power(10.0, jax.random.uniform(draw_three, (1, D), jnp.float32, 0.0, 1.0))
    return (base_draw * row_scale * col_scale * rising[None, :]).astype(jnp.bfloat16)


def with_ends(array, rng, smallest, high):
    shape = array.shape
    spot = [jax.random.randint(jax.random.fold_in(rng, axis), (), 0, shape[axis]) for axis in range(len(shape))]
    array = array.at[tuple(spot)].set(smallest)
    longest = shape.index(max(shape))
    spot[longest] = (spot[longest] + 1) % shape[longest]
    return array.at[tuple(spot)].set(high)


def block_levels(stream_key, dims, shards, low, largest):
    def one(position, parts):
        heights = jax.random.uniform(jax.random.fold_in(jax.random.fold_in(stream_key, 6), position), (parts,), jnp.float32, low / len(shards), largest / len(shards))
        return jnp.repeat(jnp.exp(heights), dims[position] // parts).reshape((-1,) + (1,) * (len(dims) - position - 1))

    factor_of = one(*shards[0])
    for cut in shards[1:]:
        factor_of = factor_of * one(*cut)
    return factor_of


def routed_block(stream_key, own, number, rows, number_of, top, limit, lean):
    order = jax.random.permutation(stream_key, number_of)
    crowded, ordinary = portions_of(number_of, rows * top, limit, lean, True), portions_of(number_of, rows * top, limit, lean, False)
    places = jnp.arange(number_of)

    def named(tallies, rotation):
        used = int((tallies > 0).sum())
        fixed = max(1, used // 4)
        passed = fixed + (places - fixed + rotation * (used - fixed)) % max(1, number_of - fixed)
        return jnp.zeros((number_of,), jnp.int32).at[order[jnp.where(places < fixed, places, passed)]].set(jnp.asarray(tallies, jnp.int32))

    tallies = jnp.where(number % 4 == 0, named(crowded, number // 4), named(ordinary, number - number // 4 - 1))
    mixed = jax.random.permutation(jax.random.fold_in(own, 3), number_of)
    source_of, taker = mixed[0:number_of // 2 * 2:2], mixed[1:number_of // 2 * 2:2]
    slack = jnp.minimum(tallies[source_of] - 1, limit - tallies[taker]) // 2
    slack = jnp.where((source_of == order[0]) | (taker == order[0]) | (tallies[taker] == 0), 0, jnp.maximum(slack, 0))
    passed = jax.random.randint(jax.random.fold_in(own, 4), (number_of // 2,), 0, 1 << 20) % (slack + 1)
    tallies = tallies.at[source_of].add(-passed).at[taker].add(passed)
    members = jnp.searchsorted(jnp.cumsum(tallies), jnp.arange(rows * top), side="right").astype(jnp.int32)
    table = members.reshape(top, rows).T
    table = table[jax.random.permutation(jax.random.fold_in(own, 1), rows)]
    rotation = jax.random.randint(jax.random.fold_in(own, 2), (rows, 1), 0, top)
    return jnp.take_along_axis(table, (jnp.arange(top)[None, :] + rotation) % top, axis=1)


def portions_of(number_of, total, bound, skew, full):
    loads = [(1 << 20) // math.isqrt(grade ** skew) + 1 for grade in range(1, number_of + 1)]
    largest = bound if full else min(bound, max(-(-total // number_of), total * loads[0] // sum(loads)))
    least = 1 if total - largest >= number_of - 1 else 0
    given, rest = [largest] + [least] * (number_of - 1), total - largest - least * (number_of - 1)
    while rest > 0:
        free = [i for i in range(1, number_of) if given[i] < largest] or [i for i in range(1, number_of) if given[i] < bound]
        whole, budget = sum([loads[i] for i in free]), rest
        for i in free:
            addition = min(bound - given[i], max(1, budget * loads[i] // whole), rest)
            given[i] = given[i] + addition
            rest = rest - addition
    return np.array(given)


def noise(own_key, shape, deviation, bound, shards=(), kind=jnp.bfloat16):
    result = jax.random.normal(own_key, shape, jnp.float32) * deviation
    if len(shards) > 0:
        result = block_levels(own_key, shape, shards, -0.22, 0.18) * result
    return jnp.clip(result, min=-bound, max=bound).astype(kind)


def setup_inputs(seed: int = 0) -> dict:
    key_of = jax.random.split(jax.random.key(seed), 12)
    hidden_state = draw_hidden_state(jax.random.fold_in(key_of[11], 71), 0)
    norm_gain = jnp.clip(1.0 + 0.18 * jax.random.normal(key_of[1], (D,), jnp.float32), 0.099609375, 1.8984375).astype(jnp.bfloat16)
    kv_weight = noise(key_of[2], (D, KVH, 2 * HD), D ** -0.5, 0.078125, ((0, 2),))
    queries = draw_queries(jax.random.fold_in(key_of[11], 71), 0)
    pool_keys = draw_pool_keys(jax.random.fold_in(key_of[11], 71), 0)
    pool_values = noise(key_of[5], (PAGES, KVH, PAGE, HD), 1.0, 6.0, ((0, 16), (1, 2)))
    page_table = draw_page_table(jax.random.fold_in(key_of[11], 71), 0)
    lengths = with_ends(jax.random.randint(key_of[7], (ROWS,), 2, MAXP * PAGE + 1), jax.random.fold_in(key_of[7], 1), 2, MAXP * PAGE).astype(jnp.int32)
    move_target_keys = jax.random.split(jax.random.fold_in(key_of[8], 1), MIGS // MIG)
    move_target_turns = jax.random.permutation(jax.random.fold_in(key_of[8], 3), MIGS // MIG)
    move_target = jax.vmap(lambda own, number: routed_block(jax.random.fold_in(key_of[8], 2), own, number, MIG, N_INST, 1, 1, 2))(move_target_keys, move_target_turns).reshape((MIGS, 1))
    move_page = with_ends(jax.random.randint(key_of[9], (MIGS,), 0, POOL), jax.random.fold_in(key_of[9], 1), 0, POOL - 1).astype(jnp.int32)
    move_request = with_ends(jax.random.randint(key_of[10], (MIGS,), 0, REQ), jax.random.fold_in(key_of[10], 1), 0, REQ - 1).astype(jnp.int32)
    return dict(hidden_state=hidden_state, norm_gain=norm_gain, kv_weight=kv_weight, queries=queries, pool_keys=pool_keys, pool_values=pool_values, page_table=page_table, lengths=lengths, move_target=move_target, move_page=move_page, move_request=move_request)


EPSILON = 1e-05
ROPE_BASE = 1000000.0
FLOOR_SCORE = -1e+30

def rotate_keys(key_rows, positions):
    half_width = key_rows.shape[-1] // 2
    freq_steps = jnp.arange(half_width, dtype=jnp.float32)
    frequency = ROPE_BASE ** (-2.0 * freq_steps / key_rows.shape[-1])
    angles = positions.astype(jnp.float32)[:, None, None] * frequency[None, None, :]
    first_half = key_rows[..., :half_width]
    second_half = key_rows[..., half_width:]
    cosine = jnp.cos(angles)
    sine_part = jnp.sin(angles)
    return jnp.concatenate([first_half * cosine - second_half * sine_part, second_half * cosine + first_half * sine_part], axis=-1)

def round_weights(weights):
    rounded = lax.optimization_barrier(weights.astype(jnp.bfloat16))
    return rounded.astype(jnp.float32)

def reference(hidden_state, norm_gain, kv_weight, queries, pool_keys, pool_values, page_table, lengths, move_target, move_page, move_request):
    group_size = QH // KVH
    scaling = 1.0 / math.sqrt(HD)
    widened = hidden_state.astype(jnp.float32)
    squares = lax.optimization_barrier(jnp.sum(widened * widened, axis=1)) / D
    inverse = lax.rsqrt(squares + EPSILON)
    normed = (widened * inverse[:, None] * norm_gain.astype(jnp.float32)[None, :]).astype(jnp.bfloat16)
    projected = jnp.dot(normed, kv_weight.reshape(D, KVH * 2 * HD), preferred_element_type=jnp.float32).reshape(ROWS, KVH, 2 * HD)
    rotated = rotate_keys(projected[:, :, :HD], lengths)
    new_kv = jnp.concatenate([rotated, projected[:, :, HD:]], axis=-1).astype(jnp.bfloat16)

    def local_part(inputs):
        query_inst, key_pool, value_pool, table_inst, length_inst, fresh_inst = inputs
        grouped = query_inst.astype(jnp.float32).reshape(REQ, KVH, group_size, HD)
        key_rows = key_pool[table_inst].astype(jnp.float32)
        value_rows = value_pool[table_inst].astype(jnp.float32)
        scores = jnp.einsum('rgqd,rigtd->rgqit', grouped, key_rows) * scaling
        token_pos = jnp.arange(MAXP, dtype=jnp.int32)[:, None] * PAGE + jnp.arange(PAGE, dtype=jnp.int32)[None, :]
        usable = (token_pos[None] < length_inst[:, None, None])[:, None, None]
        masked = jnp.where(usable, scores, FLOOR_SCORE)
        highest = lax.optimization_barrier(jnp.max(masked, axis=-1))
        weights = jnp.where(usable, jnp.exp(masked - highest[..., None]), 0.0)
        block_sum = lax.optimization_barrier(jnp.sum(weights, axis=-1))
        block_out = jnp.einsum('rgqit,rigtd->rgqid', round_weights(weights), value_rows)
        fresh_key = fresh_inst[:, :, :HD].astype(jnp.float32)
        fresh_value = fresh_inst[:, :, HD:].astype(jnp.float32)
        fresh_score = jnp.einsum('rgqd,rgd->rgq', grouped, fresh_key) * scaling
        row_best = jnp.maximum(lax.optimization_barrier(jnp.max(highest, axis=-1)), fresh_score)
        factor = jnp.exp(highest - row_best[..., None])
        fresh_factor = jnp.exp(fresh_score - row_best)
        denominator = lax.optimization_barrier(jnp.sum(factor * block_sum, axis=-1)) + fresh_factor
        numerator = lax.optimization_barrier(jnp.sum(factor[..., None] * block_out, axis=3)) + fresh_factor[..., None] * fresh_value[:, :, None, :]
        return (row_best, denominator, numerator)
    local_best, local_den, local_num = lax.map(local_part, (queries.reshape(N_INST, REQ, QH, HD), pool_keys.reshape(N_INST, POOL, KVH, PAGE, HD), pool_values.reshape(N_INST, POOL, KVH, PAGE, HD), page_table.reshape(N_INST, REQ, MAXP), lengths.reshape(N_INST, REQ), new_kv.reshape(N_INST, REQ, KVH, 2 * HD)))
    local_best = local_best.reshape(ROWS, KVH, group_size)
    local_den = local_den.reshape(ROWS, KVH, group_size)
    local_num = local_num.reshape(ROWS, KVH, group_size, HD)
    target_rows = (move_target[:, 0] * REQ + move_request).astype(jnp.int32)

    def moved_part(inputs):
        source, rows_here, pages_here = inputs
        grouped = queries[rows_here].astype(jnp.float32).reshape(MIG, KVH, group_size, HD)
        page_ids = (source * POOL + pages_here).astype(jnp.int32)
        key_page = pool_keys[page_ids].astype(jnp.float32)
        value_page = pool_values[page_ids].astype(jnp.float32)
        scores = jnp.einsum('mgqd,mgtd->mgqt', grouped, key_page) * scaling
        highest = lax.optimization_barrier(jnp.max(scores, axis=-1))
        weights = jnp.exp(scores - highest[..., None])
        block_sum = lax.optimization_barrier(jnp.sum(weights, axis=-1))
        block_out = jnp.einsum('mgqt,mgtd->mgqd', round_weights(weights), value_page)
        return (highest, block_sum, block_out)
    moved_high, moved_sum, moved_out = lax.map(moved_part, (jnp.arange(N_INST, dtype=jnp.int32), target_rows.reshape(N_INST, MIG), move_page.reshape(N_INST, MIG)))
    moved_high = moved_high.reshape(MIGS, KVH, group_size)
    moved_sum = moved_sum.reshape(MIGS, KVH, group_size)
    moved_out = moved_out.reshape(MIGS, KVH, group_size, HD)
    row_best = local_best.at[target_rows].max(moved_high)
    local_factor = jnp.exp(local_best - row_best)
    moved_factor = jnp.exp(moved_high - row_best[target_rows])
    denominator = local_den * local_factor + jnp.zeros_like(local_den).at[target_rows].add(moved_sum * moved_factor)
    numerator = local_num * local_factor[..., None] + jnp.zeros_like(local_num).at[target_rows].add(moved_out * moved_factor[..., None])
    attention_out = (numerator / denominator[..., None]).astype(jnp.bfloat16).reshape(ROWS, QH * HD)
    return (attention_out, new_kv)
```

```python
import functools
import math

import jax
import jax.numpy as jnp
from jax import lax
from jax.experimental import pallas as pl
from jax.experimental.pallas import tpu as pltpu
from jax.sharding import PartitionSpec as P

EPSILON = 1e-05
ROPE_BASE = 1000000.0
MASKED = -1e30
LOWEST = -1e20
LOG2E = math.log2(math.e)
MESH = pl.DeviceIdType.MESH
VMEM_BYTES = 56 * 1024 * 1024
F32 = jnp.float32
BF16 = jnp.bfloat16


def greet(axes):
    barrier = pltpu.get_barrier_semaphore()
    total = 0
    for axis in axes:
        size = lax.axis_size(axis)
        me = lax.axis_index(axis)

        def signal(k, carry, axis=axis, size=size, me=me):
            pl.semaphore_signal(
                barrier, inc=1, device_id={axis: lax.rem(me + k, size)}, device_id_type=MESH
            )
            return carry

        lax.fori_loop(1, size, signal, 0)
        total += size - 1
    pl.semaphore_wait(barrier, total)


def exchange(axis, source_of, landing, send, recv):
    size = lax.axis_size(axis)
    me = lax.axis_index(axis)

    def copy(k):
        peer = lax.rem(me + k, size)
        return pltpu.make_async_remote_copy(
            src_ref=source_of(peer),
            dst_ref=landing.at[me],
            send_sem=send.at[k],
            recv_sem=recv.at[k],
            device_id={axis: peer},
            device_id_type=MESH,
        )

    def arrival(k):
        peer = lax.rem(me + size - k, size)
        return pltpu.make_async_remote_copy(
            src_ref=source_of(peer),
            dst_ref=landing.at[peer],
            send_sem=send.at[k],
            recv_sem=recv.at[k],
            device_id={axis: peer},
            device_id_type=MESH,
        )

    def start():
        def step(k, carry):
            copy(k).start()
            return carry

        lax.fori_loop(1, size, step, 0)

    def wait():
        def step(k, carry):
            arrival(k).wait_recv()
            copy(k).wait_send()
            return carry

        lax.fori_loop(1, size, step, 0)

    return start, wait


def ask_kernel(
    heads, group, plan_ref, sq_ref, q_ref, qx_ref, lab_ref, sqsum_ref,
    plans, sqs, stage, asked, landed, sems_plan, sems_sq, sems_q,
):
    ni = lax.axis_size("inst")
    me = lax.axis_index("inst")
    me_tp = lax.axis_index("tp")
    greet(("inst", "tp"))
    start_plan, wait_plan = exchange("inst", lambda p: plan_ref, plans, sems_plan.at[0], sems_plan.at[1])
    start_sq, wait_sq = exchange("tp", lambda p: sq_ref, sqs, sems_sq.at[0], sems_sq.at[1])
    start_plan()
    start_sq()
    plans[me] = plan_ref[...]
    sqs[me_tp] = sq_ref[...]
    stage[...] = jnp.zeros_like(stage)
    wait_plan()
    mine = plans[:, 0, :] == me.astype(F32)
    label = jnp.sum(jnp.where(mine, plans[:, 1, :] + 1.0, 0.0), axis=1, keepdims=True) - 1.0
    lanes = lax.broadcasted_iota(jnp.int32, (ni, q_ref.shape[1]), 1).astype(F32)
    lab_ref[...] = jnp.broadcast_to(label, lab_ref.shape)
    pick = jnp.where(label == lanes, 1.0, 0.0).astype(BF16)
    for h in range(heads):
        stage[:, h, :] = jnp.dot(pick, q_ref[h], preferred_element_type=F32)
    asked[...] = stage[...].astype(BF16)
    start_q, wait_q = exchange("inst", lambda p: asked.at[p], landed, sems_q.at[0], sems_q.at[1])
    start_q()
    landed[me] = asked[me]
    wait_sq()
    sqsum_ref[...] = jnp.sum(sqs[...], axis=0)
    wait_q()
    stage[...] = landed[...].astype(F32)
    qx_ref[...] = jnp.zeros_like(qx_ref)
    for g in range(heads // group):
        for q in range(group):
            qx_ref[g, q * ni : (q + 1) * ni, :] = stage[:, g * group + q, :].astype(BF16)


def attend_kernel(
    ni, target_ref, page_ref, q_ref, qx_ref, k_ref, v_ref, pt_ref, len_ref,
    o_ref, ml_ref, vb_ref, sg_ref, lim, limx, vt, s_buf, sx_buf,
):
    pool, page, hd = k_ref.shape[0], k_ref.shape[2], k_ref.shape[3]
    group = q_ref.shape[0]
    nx = qx_ref.shape[1]
    scale = LOG2E / math.sqrt(hd)

    @pl.when(pl.program_id(0) == 0)
    def _():
        slots = pt_ref.shape[0]
        first = lax.broadcasted_iota(jnp.int32, pt_ref.shape, 0) * page
        room = jnp.clip(len_ref[...] - first, 0, page).astype(F32)
        column = lax.broadcasted_iota(jnp.int32, (1, nx), 1)
        owner = lax.rem(column, ni)
        wanted = jnp.full((1, nx), -1, jnp.int32)
        for m in range(target_ref.shape[0]):
            wanted = jnp.where(owner == target_ref[m], page_ref[m], wanted)
        wanted = jnp.where(column < group * ni, wanted, -1)
        for p in range(pool):
            lim[p : p + 1, :] = jnp.sum(
                jnp.where(pt_ref[...] == p, room, 0.0), axis=0, keepdims=True
            )
            limx[p : p + 1, :] = jnp.where(wanted == p, float(page), 0.0)
        vt[hd:, :] = jnp.ones((vt.shape[0] - hd, vt.shape[1]), BF16)

    for p in range(pool):
        vt[:hd, p * page : (p + 1) * page] = v_ref[p, 0].T
    pages = 4 if pool % 4 == 0 else 1
    span = pages * page
    chunks = pool // pages
    tokens = lax.broadcasted_iota(jnp.int32, (page, 128), 0).astype(F32)
    pair = 2 if group % 2 == 0 else 1
    tiles = [("main", j) for j in range(group // pair)] + [("extra", j) for j in range(nx // 128)]
    state = {}

    def first_pass(i, ci):
        kind, j = tiles[i]
        if kind == "main":
            qs = q_ref[j * pair : (j + 1) * pair].reshape(pair * 128, hd)
        else:
            qs = qx_ref[0, j * 128 : (j + 1) * 128, :]
        width = qs.shape[0]
        keys = k_ref[ci * pages : (ci + 1) * pages, 0].reshape(span, hd)
        s = lax.dot_general(keys, qs, (((1,), (1,)), ((), ())), preferred_element_type=F32)
        highs = state.get(i)
        if highs is None:
            highs = [jnp.full((8, 128), LOWEST, F32) for _ in range(width // 128)]
        for pp in range(pages):
            p = ci * pages + pp
            if kind == "main":
                usable = tokens < lim[p : p + 1, :]
            else:
                usable = tokens < limx[p : p + 1, j * 128 : (j + 1) * 128]
            for w in range(width // 128):
                part = jnp.where(
                    usable, s[pp * page : (pp + 1) * page, w * 128 : (w + 1) * 128], MASKED
                )
                s_buf[i % 2, p * page : (p + 1) * page, w * 128 : (w + 1) * 128] = part
                highs[w] = jnp.maximum(highs[w], jnp.max(part.reshape(page // 8, 8, 128), axis=0))
        state[i] = highs

    def second_pass(i, ci, tops, total):
        width = tops.shape[1]
        rows = slice(ci * span, (ci + 1) * span)
        weights = jnp.exp2(s_buf[i % 2, rows, :width] * scale - tops).astype(BF16)
        part = jnp.dot(vt[:, rows], weights, preferred_element_type=F32)
        return part if total is None else total + part

    for ci in range(chunks):
        first_pass(0, ci)
    for i, (kind, j) in enumerate(tiles):
        tops = jnp.concatenate(
            [jnp.max(high, axis=0, keepdims=True) for high in state[i]], axis=1
        ) * scale
        total = None
        for ci in range(chunks):
            if i + 1 < len(tiles):
                first_pass(i + 1, ci)
            total = second_pass(i, ci, tops, total)
        sums = total[hd : hd + 1, :]
        if kind == "main":
            columns = slice(j * pair * 128, (j + 1) * pair * 128)
            o_ref[0, :, columns] = total[:hd]
            ml_ref[0, 0:1, columns] = tops
            ml_ref[0, 1:2, columns] = sums
        else:
            columns = slice(j * 128, (j + 1) * 128)
            safe = jnp.maximum(sums, 1e-30)
            vb_ref[0, columns, :] = (total[:hd] / safe).T
            sg_ref[0, :, columns] = jnp.broadcast_to(tops + jnp.log(safe) * LOG2E, (8, 128))


def answer_kernel(
    heads, group, vb_ref, sg_ref, vin_ref, sin_ref,
    stage, told, table, landed, tables, sems_v, sems_s,
):
    ni = lax.axis_size("inst")
    me = lax.axis_index("inst")
    stage[...] = jnp.zeros_like(stage)
    table[...] = jnp.zeros_like(table)
    for g in range(heads // group):
        table[g : g + 1, :] = sg_ref[g, 0:1, :]
        for q in range(group):
            stage[:, g * group + q, :] = vb_ref[g, q * ni : (q + 1) * ni, :]
    told[...] = stage[...].astype(BF16)
    greet(("inst",))
    start_v, wait_v = exchange("inst", lambda p: told.at[p], landed, sems_v.at[0], sems_v.at[1])
    start_s, wait_s = exchange("inst", lambda p: table, tables, sems_s.at[0], sems_s.at[1])
    start_v()
    start_s()
    landed[me] = told[me]
    tables[me] = table[...]
    wait_v()
    wait_s()
    vin_ref[...] = landed[...].astype(F32)
    sin_ref[...] = tables[...]


def join_kernel(
    features, group, heads, me_ref, vin_ref, sin_ref, lab_ref, o_ref, ml_ref, q_ref, proj_ref,
    sq_ref, len_ref, out_ref, kv_ref,
):
    ni, nx = sin_ref.shape[0], sin_ref.shape[2]
    hd = q_ref.shape[2]
    req = q_ref.shape[1]
    half = hd // 2
    scale = LOG2E / math.sqrt(hd)
    me = me_ref[0]
    inverse = jnp.broadcast_to(lax.rsqrt(sq_ref[0:1, :] / features + EPSILON), (hd, req)).T
    lane = lax.broadcasted_iota(jnp.int32, (1, hd), 1)
    step = lax.rem(lane, half).astype(F32)
    frequency = jnp.exp(step * (-2.0 / hd * math.log(ROPE_BASE)))
    angles = jnp.broadcast_to(len_ref[...].astype(F32), (hd, req)).T * frequency
    cosine = jnp.cos(angles)
    sine = jnp.sin(angles) * jnp.where(lane < half, -1.0, 1.0)
    lanes = lax.broadcasted_iota(jnp.int32, (ni, req), 1).astype(F32)
    owned = lab_ref[...] == lanes
    columns = lax.broadcasted_iota(jnp.int32, (ni, nx), 1)
    ones = jnp.ones((8, hd), F32)
    for g in range(heads // group):
        x = proj_ref[g, :, :hd] * inverse
        rotated = (x * cosine + pltpu.roll(x, half, 1) * sine).astype(BF16)
        value = (proj_ref[g, :, hd:] * inverse).astype(BF16)
        kv_ref[:, 2 * g * hd : (2 * g + 1) * hd] = rotated
        kv_ref[:, (2 * g + 1) * hd : (2 * g + 2) * hd] = value
        key = rotated.astype(F32)
        value_t = value.astype(F32).T
        for q in range(group):
            h = g * group + q
            tile = slice(q * req, (q + 1) * req)
            fresh = lax.dot_general(
                ones, q_ref[h].astype(F32) * key, (((1,), (1,)), ((), ())),
                precision=lax.Precision.HIGHEST, preferred_element_type=F32,
            )[0:1] * scale
            level = jnp.sum(
                jnp.where(columns == q * ni + me, sin_ref[:, g, :], 0.0), axis=1, keepdims=True
            )
            moved = jnp.where(owned, level, MASKED)
            top = ml_ref[g, 0:1, tile]
            best = jnp.maximum(jnp.maximum(top, fresh), jnp.max(moved, axis=0, keepdims=True))
            local_factor = jnp.exp2(top - best)
            fresh_factor = jnp.exp2(fresh - best)
            moved_factor = jnp.where(owned, jnp.exp2(moved - best), 0.0)
            bottom = (
                local_factor * ml_ref[g, 1:2, tile]
                + fresh_factor
                + jnp.sum(moved_factor, axis=0, keepdims=True)
            )
            top_sum = (
                o_ref[g, :, tile] * local_factor
                + value_t * fresh_factor
                + lax.dot_general(
                    vin_ref[:, h, :].astype(BF16), moved_factor.astype(BF16),
                    (((0,), (0,)), ((), ())), preferred_element_type=F32,
                )
            )
            out_ref[:, h * hd : (h + 1) * hd] = (top_sum / bottom).T.astype(BF16)


def body(
    hidden_state, norm_gain, kv_weight, queries, pool_keys, pool_values,
    page_table, lengths, move_target, move_page, move_request,
):
    ni, nt = lax.axis_size("inst"), lax.axis_size("tp")
    req, heads, hd = queries.shape
    pool, key_heads, page, _ = pool_keys.shape
    group = heads // key_heads
    moves = move_page.shape[0]
    features = hidden_state.shape[1] * nt
    padded = -(-heads // 16) * 16
    nx = -(-group * ni // 128) * 128
    params = functools.partial(pltpu.CompilerParams, vmem_limit_bytes=VMEM_BYTES)
    vmem = pl.BlockSpec(memory_space=pltpu.VMEM)
    smem = pl.BlockSpec(memory_space=pltpu.SMEM)

    widened = hidden_state.astype(F32)
    squares = jnp.sum(widened * widened, axis=1)
    scaled = (widened * norm_gain.astype(F32)[None, :]).astype(BF16)
    partial = jnp.einsum("rf,fgc->grc", scaled, kv_weight, preferred_element_type=F32)
    projected = lax.psum_scatter(partial, "tp", scatter_dimension=0, tiled=True)

    by_head = jnp.transpose(queries, (1, 0, 2))
    plan = jnp.pad(
        jnp.stack([move_target[:, 0], move_request]).astype(F32),
        ((0, 6), (0, 128 - moves)),
        constant_values=-1.0,
    )
    sq_tile = jnp.broadcast_to(squares[None, :], (8, req))
    qx, label, sq_total = pl.pallas_call(
        functools.partial(ask_kernel, heads, group),
        out_shape=(
            jax.ShapeDtypeStruct((key_heads, nx, hd), BF16),
            jax.ShapeDtypeStruct((ni, req), F32),
            jax.ShapeDtypeStruct((8, req), F32),
        ),
        in_specs=[vmem] * 3,
        out_specs=(vmem,) * 3,
        scratch_shapes=[
            pltpu.VMEM((ni, 8, 128), F32),
            pltpu.VMEM((nt, 8, req), F32),
            pltpu.VMEM((ni, padded, hd), F32),
            pltpu.VMEM((ni, padded, hd), BF16),
            pltpu.VMEM((ni, padded, hd), BF16),
            pltpu.SemaphoreType.DMA((2, ni)),
            pltpu.SemaphoreType.DMA((2, nt)),
            pltpu.SemaphoreType.DMA((2, ni)),
        ],
        compiler_params=params(collective_id=0, has_side_effects=True),
        name="ask",
    )(plan, sq_tile, by_head)

    tokens = pool * page
    work = 4 * heads * (req + ni) * tokens * hd
    local, levels, moved_mean, moved_level = pl.pallas_call(
        functools.partial(attend_kernel, ni),
        grid=(key_heads,),
        out_shape=(
            jax.ShapeDtypeStruct((key_heads, hd, group * req), F32),
            jax.ShapeDtypeStruct((key_heads, 8, group * req), F32),
            jax.ShapeDtypeStruct((key_heads, nx, hd), F32),
            jax.ShapeDtypeStruct((key_heads, 8, nx), F32),
        ),
        in_specs=[
            smem,
            smem,
            pl.BlockSpec((group, req, hd), lambda g: (g, 0, 0)),
            pl.BlockSpec((1, nx, hd), lambda g: (g, 0, 0)),
            pl.BlockSpec((pool, 1, page, hd), lambda g: (0, g, 0, 0)),
            pl.BlockSpec((pool, 1, page, hd), lambda g: (0, g, 0, 0)),
            pl.BlockSpec((page_table.shape[1], req), lambda g: (0, 0)),
            pl.BlockSpec((1, req), lambda g: (0, 0)),
        ],
        out_specs=(
            pl.BlockSpec((1, hd, group * req), lambda g: (g, 0, 0)),
            pl.BlockSpec((1, 8, group * req), lambda g: (g, 0, 0)),
            pl.BlockSpec((1, nx, hd), lambda g: (g, 0, 0)),
            pl.BlockSpec((1, 8, nx), lambda g: (g, 0, 0)),
        ),
        scratch_shapes=[
            pltpu.VMEM((pool, req), F32),
            pltpu.VMEM((pool, nx), F32),
            pltpu.VMEM((hd + 16, tokens), BF16),
            pltpu.VMEM((2, tokens, 256), F32),
            pltpu.VMEM((8, 128), F32),
        ],
        compiler_params=params(),
        cost_estimate=pl.CostEstimate(
            flops=work, bytes_accessed=4 * pool_keys.size, transcendentals=heads * req * tokens
        ),
        name="attend",
    )(
        move_target[:, 0], move_page, by_head, qx, pool_keys, pool_values,
        page_table.T, lengths[None, :],
    )

    moved_in, levels_in = pl.pallas_call(
        functools.partial(answer_kernel, heads, group),
        out_shape=(
            jax.ShapeDtypeStruct((ni, padded, hd), F32),
            jax.ShapeDtypeStruct((ni, 8, nx), F32),
        ),
        in_specs=[vmem] * 2,
        out_specs=(vmem,) * 2,
        scratch_shapes=[
            pltpu.VMEM((ni, padded, hd), F32),
            pltpu.VMEM((ni, padded, hd), BF16),
            pltpu.VMEM((8, nx), F32),
            pltpu.VMEM((ni, padded, hd), BF16),
            pltpu.VMEM((ni, 8, nx), F32),
            pltpu.SemaphoreType.DMA((2, ni)),
            pltpu.SemaphoreType.DMA((2, ni)),
        ],
        compiler_params=params(collective_id=1, has_side_effects=True),
        name="answer",
    )(moved_mean, moved_level)

    me = lax.axis_index("inst").astype(jnp.int32).reshape(1)
    attention_out, new_kv = pl.pallas_call(
        functools.partial(join_kernel, features, group, heads),
        out_shape=(
            jax.ShapeDtypeStruct((req, heads * hd), BF16),
            jax.ShapeDtypeStruct((req, key_heads * 2 * hd), BF16),
        ),
        in_specs=[smem] + [vmem] * 9,
        out_specs=(vmem,) * 2,
        compiler_params=params(),
        name="join",
    )(
        me, moved_in, levels_in, label, local, levels, by_head, projected, sq_total,
        lengths[None, :],
    )
    return (attention_out, new_kv.reshape(req, key_heads, 2 * hd))


def solution(mesh):
    return jax.shard_map(
        body,
        mesh=mesh,
        in_specs=(
            P("inst", "tp"),
            P("tp"),
            P("tp", None, None),
            P("inst", "tp", None),
            P("inst", "tp", None, None),
            P("inst", "tp", None, None),
            P("inst", None),
            P("inst"),
            P("inst", None),
            P("inst"),
            P("inst"),
        ),
        out_specs=(P("inst", "tp"), P("inst", "tp", None)),
        check_vma=False,
    )
```

```python
import functools
import math

import jax
import jax.numpy as jnp
from jax import lax
from jax.experimental import pallas as pl
from jax.experimental.pallas import tpu as pltpu
from jax.sharding import PartitionSpec as P

EPSILON = 1e-05
ROPE_BASE = 1000000.0
MASKED = -1e30
LOWEST = -1e20
LOG2E = math.log2(math.e)
MESH = pl.DeviceIdType.MESH
VMEM_BYTES = 56 * 1024 * 1024
F32 = jnp.float32
BF16 = jnp.bfloat16


def greet(axes):
    barrier = pltpu.get_barrier_semaphore()
    total = 0
    for axis in axes:
        size = lax.axis_size(axis)
        me = lax.axis_index(axis)

        def signal(k, carry, axis=axis, size=size, me=me):
            pl.semaphore_signal(
                barrier, inc=1, device_id={axis: lax.rem(me + k, size)}, device_id_type=MESH
            )
            return carry

        lax.fori_loop(1, size, signal, 0)
        total += size - 1
    pl.semaphore_wait(barrier, total)


def exchange(axis, source_of, landing, send, recv):
    size = lax.axis_size(axis)
    me = lax.axis_index(axis)

    def copy(k):
        peer = lax.rem(me + k, size)
        return pltpu.make_async_remote_copy(
            src_ref=source_of(peer),
            dst_ref=landing.at[me],
            send_sem=send.at[k],
            recv_sem=recv.at[k],
            device_id={axis: peer},
            device_id_type=MESH,
        )

    def arrival(k):
        peer = lax.rem(me + size - k, size)
        return pltpu.make_async_remote_copy(
            src_ref=source_of(peer),
            dst_ref=landing.at[peer],
            send_sem=send.at[k],
            recv_sem=recv.at[k],
            device_id={axis: peer},
            device_id_type=MESH,
        )

    def start():
        def step(k, carry):
            copy(k).start()
            return carry

        lax.fori_loop(1, size, step, 0)

    def wait():
        def step(k, carry):
            arrival(k).wait_recv()
            copy(k).wait_send()
            return carry

        lax.fori_loop(1, size, step, 0)

    return start, wait


def attend_kernel(
    heads, group, plan_ref, sq_ref, target_ref, page_ref, q_ref, pt_ref, len_ref, k_hbm, v_hbm,
    o_ref, ml_ref, lab_ref, sqsum_ref, vin_ref, sin_ref,
    keys, values, lim, limx, vt, s_buf, qx, stage, asked, queried, told, told_in,
    plans, sqs, table, tables, sems_kv, sems_plan, sems_sq, sems_q, sems_v, sems_s,
):
    ni = lax.axis_size("inst")
    me = lax.axis_index("inst")
    me_tp = lax.axis_index("tp")
    key_heads, pool, page, hd = keys.shape
    req = q_ref.shape[1]
    nx = qx.shape[1]
    scale = LOG2E / math.sqrt(hd)

    def fetch(g, which):
        source, target = ((k_hbm, keys), (v_hbm, values))[which]
        return pltpu.make_async_copy(source.at[:, g], target.at[g], sems_kv.at[which, g])

    for g in range(key_heads):
        fetch(g, 0).start()
        fetch(g, 1).start()
    greet(("inst", "tp"))
    start_plan, wait_plan = exchange("inst", lambda p: plan_ref, plans, sems_plan.at[0], sems_plan.at[1])
    start_sq, wait_sq = exchange("tp", lambda p: sq_ref, sqs, sems_sq.at[0], sems_sq.at[1])
    start_q, wait_q = exchange("inst", lambda p: asked.at[p], queried, sems_q.at[0], sems_q.at[1])
    start_v, wait_v = exchange("inst", lambda p: told.at[p], told_in, sems_v.at[0], sems_v.at[1])
    start_s, wait_s = exchange("inst", lambda p: table, tables, sems_s.at[0], sems_s.at[1])
    start_plan()
    start_sq()
    plans[me] = plan_ref[...]
    sqs[me_tp] = sq_ref[...]

    first = lax.broadcasted_iota(jnp.int32, pt_ref.shape, 0) * page
    room = jnp.clip(len_ref[...] - first, 0, page).astype(F32)
    column = lax.broadcasted_iota(jnp.int32, (1, nx), 1)
    owner = lax.rem(column, ni)
    wanted = jnp.full((1, nx), -1, jnp.int32)
    for m in range(target_ref.shape[0]):
        wanted = jnp.where(owner == target_ref[m], page_ref[m], wanted)
    wanted = jnp.where(column < group * ni, wanted, -1)
    for p in range(pool):
        lim[p : p + 1, :] = jnp.sum(jnp.where(pt_ref[...] == p, room, 0.0), axis=0, keepdims=True)
        limx[p : p + 1, :] = jnp.where(wanted == p, float(page), 0.0)
    vt[:, hd:, :] = jnp.ones((key_heads, vt.shape[1] - hd, vt.shape[2]), BF16)
    stage[...] = jnp.zeros_like(stage)
    table[...] = jnp.zeros_like(table)
    qx[...] = jnp.zeros_like(qx)

    pages = 4 if pool % 4 == 0 else 1
    span = pages * page
    chunks = pool // pages
    tokens = lax.broadcasted_iota(jnp.int32, (page, 128), 0).astype(F32)
    pair = 2 if group % 2 == 0 else 1

    def attend(g, blocks, limits, finish):
        state = {}

        def first_pass(i, ci):
            qs = blocks[i]()
            width = qs.shape[0]
            rows = keys[g, ci * pages : (ci + 1) * pages].reshape(span, hd)
            s = lax.dot_general(rows, qs, (((1,), (1,)), ((), ())), preferred_element_type=F32)
            highs = state.get(i)
            if highs is None:
                highs = [jnp.full((8, 128), LOWEST, F32) for _ in range(width // 128)]
            for pp in range(pages):
                p = ci * pages + pp
                usable = tokens < limits(i, p)
                for w in range(width // 128):
                    part = jnp.where(
                        usable, s[pp * page : (pp + 1) * page, w * 128 : (w + 1) * 128], MASKED
                    )
                    s_buf[i % 2, p * page : (p + 1) * page, w * 128 : (w + 1) * 128] = part
                    high = jnp.max(part.reshape(page // 8, 8, 128), axis=0)
                    highs[w] = jnp.maximum(highs[w], high)
            state[i] = highs

        for ci in range(chunks):
            first_pass(0, ci)
        for i in range(len(blocks)):
            tops = jnp.concatenate(
                [jnp.max(high, axis=0, keepdims=True) for high in state[i]], axis=1
            ) * scale
            total = None
            for ci in range(chunks):
                if i + 1 < len(blocks):
                    first_pass(i + 1, ci)
                rows = slice(ci * span, (ci + 1) * span)
                weights = jnp.exp2(s_buf[i % 2, rows, : tops.shape[1]] * scale - tops)
                part = jnp.dot(vt[g, :, rows], weights.astype(BF16), preferred_element_type=F32)
                total = part if total is None else total + part
            finish(i, total[:hd], total[hd : hd + 1, :], tops)

    def attend_own(g):
        def finish(i, total, sums, tops):
            columns = slice(i * pair * 128, (i + 1) * pair * 128)
            o_ref[g, :, columns] = total
            ml_ref[g, 0:1, columns] = tops
            ml_ref[g, 1:2, columns] = sums

        blocks = [
            lambda j=j: q_ref[pl.ds(g * group + j * pair, pair)].reshape(pair * req, hd)
            for j in range(group // pair)
        ]
        attend(g, blocks, lambda i, p: lim[p : p + 1, :], finish)

    def attend_asked(g):
        def finish(j, total, sums, tops):
            safe = jnp.maximum(sums, 1e-30)
            mean = (total / safe).T
            for q in range(group):
                lo = max(q * ni, j * 128)
                hi = min((q + 1) * ni, (j + 1) * 128)
                if lo < hi:
                    stage[lo - q * ni : hi - q * ni, g * group + q, :] = mean[lo - j * 128 : hi - j * 128]
            level = tops + jnp.log(safe) * LOG2E
            table[g : g + 1, j * 128 : (j + 1) * 128] = level

        blocks = [lambda j=j: qx[g, j * 128 : (j + 1) * 128, :] for j in range(nx // 128)]
        attend(g, blocks, lambda j, p: limx[p : p + 1, j * 128 : (j + 1) * 128], finish)

    def turn_values(g):
        for p in range(pool):
            vt[g, :hd, p * page : (p + 1) * page] = values[g, p].T

    def ask():
        wait_plan()
        mine = plans[:, 0, :] == me.astype(F32)
        label = jnp.sum(jnp.where(mine, plans[:, 1, :] + 1.0, 0.0), axis=1, keepdims=True) - 1.0
        lanes = lax.broadcasted_iota(jnp.int32, (ni, req), 1).astype(F32)
        lab_ref[...] = jnp.broadcast_to(label, lab_ref.shape)
        pick = jnp.where(label == lanes, 1.0, 0.0).astype(BF16)
        for h in range(heads):
            stage[:, h, :] = jnp.dot(pick, q_ref[h], preferred_element_type=F32)
        asked[...] = stage[...].astype(BF16)
        start_q()
        queried[me] = asked[me]

    def answer():
        wait_q()
        stage[...] = queried[...].astype(F32)
        for g in range(key_heads):
            for q in range(group):
                qx[g, q * ni : (q + 1) * ni, :] = stage[:, g * group + q, :].astype(BF16)
        for g in range(key_heads):
            attend_asked(g)
        told[...] = stage[...].astype(BF16)
        start_v()
        start_s()
        told_in[me] = told[me]
        tables[me] = table[...]

    def own(g, carry):
        for which in range(2):
            fetch(g, which).wait()
        turn_values(g)
        attend_own(g)

        @pl.when(g == 0)
        def _():
            ask()

        return carry

    early = min(2, key_heads)
    lax.fori_loop(0, early, own, 0)
    for g in range(early, key_heads):
        for which in range(2):
            fetch(g, which).wait()
        turn_values(g)
    answer()

    def rest(g, carry):
        attend_own(g)
        return carry

    lax.fori_loop(early, key_heads, rest, 0)
    wait_sq()
    sqsum_ref[...] = jnp.sum(sqs[...], axis=0)
    wait_v()
    wait_s()
    vin_ref[...] = told_in[...].astype(F32)
    sin_ref[...] = tables[...]


def join_kernel(
    features, group, heads, me_ref, vin_ref, sin_ref, lab_ref, o_ref, ml_ref, q_ref, proj_ref,
    sq_ref, len_ref, out_ref, kv_ref,
):
    ni, nx = sin_ref.shape[0], sin_ref.shape[2]
    hd = q_ref.shape[2]
    req = q_ref.shape[1]
    half = hd // 2
    scale = LOG2E / math.sqrt(hd)
    me = me_ref[0]
    inverse = jnp.broadcast_to(lax.rsqrt(sq_ref[0:1, :] / features + EPSILON), (hd, req)).T
    lane = lax.broadcasted_iota(jnp.int32, (1, hd), 1)
    step = lax.rem(lane, half).astype(F32)
    frequency = jnp.exp(step * (-2.0 / hd * math.log(ROPE_BASE)))
    angles = jnp.broadcast_to(len_ref[...].astype(F32), (hd, req)).T * frequency
    cosine = jnp.cos(angles)
    sine = jnp.sin(angles) * jnp.where(lane < half, -1.0, 1.0)
    lanes = lax.broadcasted_iota(jnp.int32, (ni, req), 1).astype(F32)
    owned = lab_ref[...] == lanes
    columns = lax.broadcasted_iota(jnp.int32, (ni, nx), 1)
    ones = jnp.ones((16, 3 * hd), BF16)
    for g in range(heads // group):
        x = proj_ref[g, :, :hd] * inverse
        rotated = (x * cosine + pltpu.roll(x, half, 1) * sine).astype(BF16)
        value = (proj_ref[g, :, hd:] * inverse).astype(BF16)
        kv_ref[:, 2 * g * hd : (2 * g + 1) * hd] = rotated
        kv_ref[:, (2 * g + 1) * hd : (2 * g + 2) * hd] = value
        key = rotated.astype(F32)
        value_t = value.astype(F32).T
        for q in range(group):
            h = g * group + q
            tile = slice(q * req, (q + 1) * req)
            product = q_ref[h].astype(F32) * key
            high = product.astype(BF16)
            rest = product - high.astype(F32)
            middle = rest.astype(BF16)
            low = (rest - middle.astype(F32)).astype(BF16)
            fresh = lax.dot_general(
                ones, jnp.concatenate([high, middle, low], axis=1), (((1,), (1,)), ((), ())),
                preferred_element_type=F32,
            )[0:1] * scale
            level = jnp.sum(
                jnp.where(columns == q * ni + me, sin_ref[:, g, :], 0.0), axis=1, keepdims=True
            )
            moved = jnp.where(owned, level, MASKED)
            top = ml_ref[g, 0:1, tile]
            best = jnp.maximum(jnp.maximum(top, fresh), jnp.max(moved, axis=0, keepdims=True))
            local_factor = jnp.exp2(top - best)
            fresh_factor = jnp.exp2(fresh - best)
            moved_factor = jnp.where(owned, jnp.exp2(moved - best), 0.0)
            bottom = (
                local_factor * ml_ref[g, 1:2, tile]
                + fresh_factor
                + jnp.sum(moved_factor, axis=0, keepdims=True)
            )
            top_sum = (
                o_ref[g, :, tile] * local_factor
                + value_t * fresh_factor
                + lax.dot_general(
                    vin_ref[:, h, :].astype(BF16), moved_factor.astype(BF16),
                    (((0,), (0,)), ((), ())), preferred_element_type=F32,
                )
            )
            out_ref[:, h * hd : (h + 1) * hd] = (top_sum / bottom).T.astype(BF16)


def body(
    hidden_state, norm_gain, kv_weight, queries, pool_keys, pool_values,
    page_table, lengths, move_target, move_page, move_request,
):
    ni, nt = lax.axis_size("inst"), lax.axis_size("tp")
    req, heads, hd = queries.shape
    pool, key_heads, page, _ = pool_keys.shape
    group = heads // key_heads
    moves = move_page.shape[0]
    features = hidden_state.shape[1] * nt
    padded = -(-heads // 16) * 16
    nx = -(-group * ni // 128) * 128
    params = functools.partial(pltpu.CompilerParams, vmem_limit_bytes=VMEM_BYTES)
    vmem = pl.BlockSpec(memory_space=pltpu.VMEM)
    smem = pl.BlockSpec(memory_space=pltpu.SMEM)

    widened = hidden_state.astype(F32)
    squares = jnp.sum(widened * widened, axis=1)
    scaled = (widened * norm_gain.astype(F32)[None, :]).astype(BF16)
    partial = jnp.einsum("rf,fgc->grc", scaled, kv_weight, preferred_element_type=F32)
    projected = lax.psum_scatter(partial, "tp", scatter_dimension=0, tiled=True)

    by_head = jnp.transpose(queries, (1, 0, 2))
    plan = jnp.pad(
        jnp.stack([move_target[:, 0], move_request]).astype(F32),
        ((0, 6), (0, 128 - moves)),
        constant_values=-1.0,
    )
    sq_tile = jnp.broadcast_to(squares[None, :], (8, req))
    tokens = pool * page
    slots = pltpu.VMEM((ni, padded, hd), BF16)
    hbm = pl.BlockSpec(memory_space=pl.ANY)
    local, levels, label, sq_total, moved_in, levels_in = pl.pallas_call(
        functools.partial(attend_kernel, heads, group),
        out_shape=(
            jax.ShapeDtypeStruct((key_heads, hd, group * req), F32),
            jax.ShapeDtypeStruct((key_heads, 8, group * req), F32),
            jax.ShapeDtypeStruct((ni, req), F32),
            jax.ShapeDtypeStruct((8, req), F32),
            jax.ShapeDtypeStruct((ni, padded, hd), F32),
            jax.ShapeDtypeStruct((ni, 8, nx), F32),
        ),
        in_specs=[vmem, vmem, smem, smem, vmem, vmem, vmem, hbm, hbm],
        out_specs=(vmem,) * 6,
        scratch_shapes=[
            pltpu.VMEM((key_heads, pool, page, hd), BF16),
            pltpu.VMEM((key_heads, pool, page, hd), BF16),
            pltpu.VMEM((pool, req), F32),
            pltpu.VMEM((pool, nx), F32),
            pltpu.VMEM((key_heads, hd + 16, tokens), BF16),
            pltpu.VMEM((2, tokens, 256), F32),
            pltpu.VMEM((key_heads, nx, hd), BF16),
            pltpu.VMEM((ni, padded, hd), F32),
            slots,
            slots,
            slots,
            slots,
            pltpu.VMEM((ni, 8, 128), F32),
            pltpu.VMEM((nt, 8, req), F32),
            pltpu.VMEM((8, nx), F32),
            pltpu.VMEM((ni, 8, nx), F32),
            pltpu.SemaphoreType.DMA((2, key_heads)),
            pltpu.SemaphoreType.DMA((2, ni)),
            pltpu.SemaphoreType.DMA((2, nt)),
            pltpu.SemaphoreType.DMA((2, ni)),
            pltpu.SemaphoreType.DMA((2, ni)),
            pltpu.SemaphoreType.DMA((2, ni)),
        ],
        compiler_params=params(collective_id=0, has_side_effects=True),
        cost_estimate=pl.CostEstimate(
            flops=4 * heads * (req + ni) * tokens * hd,
            bytes_accessed=4 * pool_keys.size,
            transcendentals=heads * req * tokens,
        ),
        name="attend",
    )(
        plan, sq_tile, move_target[:, 0], move_page, by_head, page_table.T, lengths[None, :],
        pool_keys, pool_values,
    )

    me = lax.axis_index("inst").astype(jnp.int32).reshape(1)
    attention_out, new_kv = pl.pallas_call(
        functools.partial(join_kernel, features, group, heads),
        out_shape=(
            jax.ShapeDtypeStruct((req, heads * hd), BF16),
            jax.ShapeDtypeStruct((req, key_heads * 2 * hd), BF16),
        ),
        in_specs=[smem] + [vmem] * 9,
        out_specs=(vmem,) * 2,
        compiler_params=params(),
        name="join",
    )(
        me, moved_in, levels_in, label, local, levels, by_head, projected, sq_total,
        lengths[None, :],
    )
    return (attention_out, new_kv.reshape(req, key_heads, 2 * hd))


def solution(mesh):
    return jax.shard_map(
        body,
        mesh=mesh,
        in_specs=(
            P("inst", "tp"),
            P("tp"),
            P("tp", None, None),
            P("inst", "tp", None),
            P("inst", "tp", None, None),
            P("inst", "tp", None, None),
            P("inst", None),
            P("inst"),
            P("inst", None),
            P("inst"),
            P("inst"),
        ),
        out_specs=(P("inst", "tp"), P("inst", "tp", None)),
        check_vma=False,
    )
```

```python
import functools
import math

import jax
import jax.numpy as jnp
from jax import lax
from jax.experimental import pallas as pl
from jax.experimental.pallas import tpu as pltpu
from jax.sharding import PartitionSpec as P

EPSILON = 1e-05
ROPE_BASE = 1000000.0
MASKED = -1e30
LOWEST = -1e20
LOG2E = math.log2(math.e)
MESH = pl.DeviceIdType.MESH
VMEM_BYTES = 56 * 1024 * 1024
F32 = jnp.float32
BF16 = jnp.bfloat16


def greet(axes):
    barrier = pltpu.get_barrier_semaphore()
    total = 0
    for axis in axes:
        size = lax.axis_size(axis)
        me = lax.axis_index(axis)

        def signal(k, carry, axis=axis, size=size, me=me):
            pl.semaphore_signal(
                barrier, inc=1, device_id={axis: lax.rem(me + k, size)}, device_id_type=MESH
            )
            return carry

        lax.fori_loop(1, size, signal, 0)
        total += size - 1
    pl.semaphore_wait(barrier, total)


def exchange(axis, source_of, landing, send, recv):
    size = lax.axis_size(axis)
    me = lax.axis_index(axis)

    def copy(k):
        peer = lax.rem(me + k, size)
        return pltpu.make_async_remote_copy(
            src_ref=source_of(peer),
            dst_ref=landing.at[me],
            send_sem=send.at[k],
            recv_sem=recv.at[k],
            device_id={axis: peer},
            device_id_type=MESH,
        )

    def arrival(k):
        peer = lax.rem(me + size - k, size)
        return pltpu.make_async_remote_copy(
            src_ref=source_of(peer),
            dst_ref=landing.at[peer],
            send_sem=send.at[k],
            recv_sem=recv.at[k],
            device_id={axis: peer},
            device_id_type=MESH,
        )

    def start():
        def step(k, carry):
            copy(k).start()
            return carry

        lax.fori_loop(1, size, step, 0)

    def wait():
        def step(k, carry):
            arrival(k).wait_recv()
            copy(k).wait_send()
            return carry

        lax.fori_loop(1, size, step, 0)

    return start, wait


def attend_kernel(
    heads, group, to_ref, asks_ref, squares_ref, target_ref, page_ref, q_ref, pt_ref, len_ref, k_hbm, v_hbm,
    o_ref, ml_ref, lab_ref, sqsum_ref, vin_ref, sin_ref,
    keys, values, lim, limx, vt, s_buf, qx, stage, asked, queried, told, told_in,
    plan_ref, sq_ref, plans, sqs, table, tables, sems_kv, sems_plan, sems_sq, sems_q, sems_v, sems_s,
):
    ni = lax.axis_size("inst")
    me = lax.axis_index("inst")
    me_tp = lax.axis_index("tp")
    key_heads, pool, page, hd = keys.shape
    req = q_ref.shape[1]
    nx = qx.shape[1]
    scale = LOG2E / math.sqrt(hd)

    def fetch(g, which):
        source, target = ((k_hbm, keys), (v_hbm, values))[which]
        return pltpu.make_async_copy(source.at[:, g], target.at[g], sems_kv.at[which, g])

    for g in range(key_heads):
        fetch(g, 0).start()
        fetch(g, 1).start()
    moves = to_ref.shape[1]
    plan_ref[...] = jnp.full(plan_ref.shape, -1.0, F32)
    plan_ref[0:1, :moves] = to_ref[...].astype(F32)
    plan_ref[1:2, :moves] = asks_ref[...].astype(F32)
    sq_ref[...] = jnp.broadcast_to(squares_ref[...], sq_ref.shape)
    greet(("inst", "tp"))
    start_plan, wait_plan = exchange("inst", lambda p: plan_ref, plans, sems_plan.at[0], sems_plan.at[1])
    start_sq, wait_sq = exchange("tp", lambda p: sq_ref, sqs, sems_sq.at[0], sems_sq.at[1])
    start_q, wait_q = exchange("inst", lambda p: asked.at[p], queried, sems_q.at[0], sems_q.at[1])
    start_v, wait_v = exchange("inst", lambda p: told.at[p], told_in, sems_v.at[0], sems_v.at[1])
    start_s, wait_s = exchange("inst", lambda p: table, tables, sems_s.at[0], sems_s.at[1])
    start_plan()
    start_sq()
    plans[me] = plan_ref[...]
    sqs[me_tp] = sq_ref[...]

    first = lax.broadcasted_iota(jnp.int32, pt_ref.shape, 0) * page
    room = jnp.clip(len_ref[...] - first, 0, page).astype(F32)
    column = lax.broadcasted_iota(jnp.int32, (1, nx), 1)
    owner = lax.rem(column, ni)
    wanted = jnp.full((1, nx), -1, jnp.int32)
    for m in range(target_ref.shape[0]):
        wanted = jnp.where(owner == target_ref[m], page_ref[m], wanted)
    wanted = jnp.where(column < group * ni, wanted, -1)
    for p in range(pool):
        lim[p : p + 1, :] = jnp.sum(jnp.where(pt_ref[...] == p, room, 0.0), axis=0, keepdims=True)
        limx[p : p + 1, :] = jnp.where(wanted == p, float(page), 0.0)
    vt[:, hd:, :] = jnp.ones((key_heads, vt.shape[1] - hd, vt.shape[2]), BF16)
    stage[...] = jnp.zeros_like(stage)
    table[...] = jnp.zeros_like(table)
    qx[...] = jnp.zeros_like(qx)

    pages = 4 if pool % 4 == 0 else 1
    span = pages * page
    chunks = pool // pages
    tokens = lax.broadcasted_iota(jnp.int32, (page, 128), 0).astype(F32)
    pair = 2 if group % 2 == 0 else 1

    def attend(g, blocks, limits, finish):
        state = {}

        def first_pass(i, ci):
            qs = blocks[i]()
            width = qs.shape[0]
            rows = keys[g, ci * pages : (ci + 1) * pages].reshape(span, hd)
            s = lax.dot_general(rows, qs, (((1,), (1,)), ((), ())), preferred_element_type=F32)
            highs = state.get(i)
            if highs is None:
                highs = [jnp.full((8, 128), LOWEST, F32) for _ in range(width // 128)]
            for pp in range(pages):
                p = ci * pages + pp
                usable = tokens < limits(i, p)
                for w in range(width // 128):
                    part = jnp.where(
                        usable, s[pp * page : (pp + 1) * page, w * 128 : (w + 1) * 128], MASKED
                    )
                    s_buf[i % 2, p * page : (p + 1) * page, w * 128 : (w + 1) * 128] = part
                    high = jnp.max(part.reshape(page // 8, 8, 128), axis=0)
                    highs[w] = jnp.maximum(highs[w], high)
            state[i] = highs

        for ci in range(chunks):
            first_pass(0, ci)
        for i in range(len(blocks)):
            tops = jnp.concatenate(
                [jnp.max(high, axis=0, keepdims=True) for high in state[i]], axis=1
            ) * scale
            total = None
            for ci in range(chunks):
                if i + 1 < len(blocks):
                    first_pass(i + 1, ci)
                rows = slice(ci * span, (ci + 1) * span)
                weights = jnp.exp2(s_buf[i % 2, rows, : tops.shape[1]] * scale - tops)
                part = jnp.dot(vt[g, :, rows], weights.astype(BF16), preferred_element_type=F32)
                total = part if total is None else total + part
            finish(i, total[:hd], total[hd : hd + 1, :], tops)

    def attend_own(g):
        def finish(i, total, sums, tops):
            columns = slice(i * pair * 128, (i + 1) * pair * 128)
            o_ref[g, :, columns] = total
            ml_ref[g, 0:1, columns] = tops
            ml_ref[g, 1:2, columns] = sums

        blocks = [
            lambda j=j: q_ref[pl.ds(g * group + j * pair, pair)].reshape(pair * req, hd)
            for j in range(group // pair)
        ]
        attend(g, blocks, lambda i, p: lim[p : p + 1, :], finish)

    def attend_asked(g):
        def finish(j, total, sums, tops):
            safe = jnp.maximum(sums, 1e-30)
            mean = (total / safe).T
            for q in range(group):
                lo = max(q * ni, j * 128)
                hi = min((q + 1) * ni, (j + 1) * 128)
                if lo < hi:
                    stage[lo - q * ni : hi - q * ni, g * group + q, :] = mean[lo - j * 128 : hi - j * 128]
            level = tops + jnp.log(safe) * LOG2E
            table[g : g + 1, j * 128 : (j + 1) * 128] = level

        blocks = [lambda j=j: qx[g, j * 128 : (j + 1) * 128, :] for j in range(nx // 128)]
        attend(g, blocks, lambda j, p: limx[p : p + 1, j * 128 : (j + 1) * 128], finish)

    def turn_values(g):
        for p in range(pool):
            vt[g, :hd, p * page : (p + 1) * page] = values[g, p].T

    def ask():
        wait_plan()
        mine = plans[:, 0, :] == me.astype(F32)
        label = jnp.sum(jnp.where(mine, plans[:, 1, :] + 1.0, 0.0), axis=1, keepdims=True) - 1.0
        lanes = lax.broadcasted_iota(jnp.int32, (ni, req), 1).astype(F32)
        lab_ref[...] = jnp.broadcast_to(label, lab_ref.shape)
        pick = jnp.where(label == lanes, 1.0, 0.0).astype(BF16)
        for h in range(heads):
            stage[:, h, :] = jnp.dot(pick, q_ref[h], preferred_element_type=F32)
        asked[...] = stage[...].astype(BF16)
        start_q()
        queried[me] = asked[me]

    def answer():
        wait_q()
        stage[...] = queried[...].astype(F32)
        for g in range(key_heads):
            for q in range(group):
                qx[g, q * ni : (q + 1) * ni, :] = stage[:, g * group + q, :].astype(BF16)
        for g in range(key_heads):
            attend_asked(g)
        told[...] = stage[...].astype(BF16)
        start_v()
        start_s()
        told_in[me] = told[me]
        tables[me] = table[...]

    def own(g, carry):
        for which in range(2):
            fetch(g, which).wait()
        turn_values(g)
        attend_own(g)

        @pl.when(g == 0)
        def _():
            ask()

        return carry

    early = min(2, key_heads)
    lax.fori_loop(0, early, own, 0)
    for g in range(early, key_heads):
        for which in range(2):
            fetch(g, which).wait()
        turn_values(g)
    answer()

    def rest(g, carry):
        attend_own(g)
        return carry

    lax.fori_loop(early, key_heads, rest, 0)
    wait_sq()
    sqsum_ref[...] = jnp.sum(sqs[...], axis=0)
    wait_v()
    wait_s()
    vin_ref[...] = told_in[...].astype(F32)
    sin_ref[...] = tables[...]


def join_kernel(
    features, group, heads, me_ref, vin_ref, sin_ref, lab_ref, o_ref, ml_ref, q_ref, proj_ref,
    sq_ref, len_ref, out_ref, kv_ref,
):
    ni, nx = sin_ref.shape[0], sin_ref.shape[2]
    hd = q_ref.shape[2]
    req = q_ref.shape[1]
    half = hd // 2
    scale = LOG2E / math.sqrt(hd)
    me = me_ref[0]
    inverse = jnp.broadcast_to(lax.rsqrt(sq_ref[0:1, :] / features + EPSILON), (hd, req)).T
    lane = lax.broadcasted_iota(jnp.int32, (1, hd), 1)
    step = lax.rem(lane, half).astype(F32)
    frequency = jnp.exp(step * (-2.0 / hd * math.log(ROPE_BASE)))
    angles = jnp.broadcast_to(len_ref[...].astype(F32), (hd, req)).T * frequency
    cosine = jnp.cos(angles)
    sine = jnp.sin(angles) * jnp.where(lane < half, -1.0, 1.0)
    lanes = lax.broadcasted_iota(jnp.int32, (ni, req), 1).astype(F32)
    owned = lab_ref[...] == lanes
    columns = lax.broadcasted_iota(jnp.int32, (ni, nx), 1)
    ones = jnp.ones((16, 3 * hd), BF16)
    for g in range(heads // group):
        x = proj_ref[g, :, :hd] * inverse
        rotated = (x * cosine + pltpu.roll(x, half, 1) * sine).astype(BF16)
        value = (proj_ref[g, :, hd:] * inverse).astype(BF16)
        kv_ref[:, 2 * g * hd : (2 * g + 1) * hd] = rotated
        kv_ref[:, (2 * g + 1) * hd : (2 * g + 2) * hd] = value
        key = rotated.astype(F32)
        value_t = value.astype(F32).T
        for q in range(group):
            h = g * group + q
            tile = slice(q * req, (q + 1) * req)
            product = q_ref[h].astype(F32) * key
            high = product.astype(BF16)
            rest = product - high.astype(F32)
            middle = rest.astype(BF16)
            low = (rest - middle.astype(F32)).astype(BF16)
            fresh = lax.dot_general(
                ones, jnp.concatenate([high, middle, low], axis=1), (((1,), (1,)), ((), ())),
                preferred_element_type=F32,
            )[0:1] * scale
            level = jnp.sum(
                jnp.where(columns == q * ni + me, sin_ref[:, g, :], 0.0), axis=1, keepdims=True
            )
            moved = jnp.where(owned, level, MASKED)
            top = ml_ref[g, 0:1, tile]
            best = jnp.maximum(jnp.maximum(top, fresh), jnp.max(moved, axis=0, keepdims=True))
            local_factor = jnp.exp2(top - best)
            fresh_factor = jnp.exp2(fresh - best)
            moved_factor = jnp.where(owned, jnp.exp2(moved - best), 0.0)
            bottom = (
                local_factor * ml_ref[g, 1:2, tile]
                + fresh_factor
                + jnp.sum(moved_factor, axis=0, keepdims=True)
            )
            top_sum = (
                o_ref[g, :, tile] * local_factor
                + value_t * fresh_factor
                + lax.dot_general(
                    vin_ref[:, h, :].astype(BF16), moved_factor.astype(BF16),
                    (((0,), (0,)), ((), ())), preferred_element_type=F32,
                )
            )
            out_ref[:, h * hd : (h + 1) * hd] = (top_sum / bottom).T.astype(BF16)


def body(
    hidden_state, norm_gain, kv_weight, queries, pool_keys, pool_values,
    page_table, lengths, move_target, move_page, move_request,
):
    ni, nt = lax.axis_size("inst"), lax.axis_size("tp")
    req, heads, hd = queries.shape
    pool, key_heads, page, _ = pool_keys.shape
    group = heads // key_heads
    features = hidden_state.shape[1] * nt
    padded = -(-heads // 16) * 16
    nx = -(-group * ni // 128) * 128
    params = functools.partial(pltpu.CompilerParams, vmem_limit_bytes=VMEM_BYTES)
    vmem = pl.BlockSpec(memory_space=pltpu.VMEM)
    smem = pl.BlockSpec(memory_space=pltpu.SMEM)

    widened = hidden_state.astype(F32)
    squares = jnp.sum(widened * widened, axis=1)
    scaled = (widened * norm_gain.astype(F32)[None, :]).astype(BF16)
    partial = jnp.einsum("rf,fgc->grc", scaled, kv_weight, preferred_element_type=F32)
    projected = lax.psum_scatter(partial, "tp", scatter_dimension=0, tiled=True)

    by_head = jnp.transpose(queries, (1, 0, 2))
    tokens = pool * page
    slots = pltpu.VMEM((ni, padded, hd), BF16)
    hbm = pl.BlockSpec(memory_space=pl.ANY)
    local, levels, label, sq_total, moved_in, levels_in = pl.pallas_call(
        functools.partial(attend_kernel, heads, group),
        out_shape=(
            jax.ShapeDtypeStruct((key_heads, hd, group * req), F32),
            jax.ShapeDtypeStruct((key_heads, 8, group * req), F32),
            jax.ShapeDtypeStruct((ni, req), F32),
            jax.ShapeDtypeStruct((8, req), F32),
            jax.ShapeDtypeStruct((ni, padded, hd), F32),
            jax.ShapeDtypeStruct((ni, 8, nx), F32),
        ),
        in_specs=[vmem, vmem, vmem, smem, smem, vmem, vmem, vmem, hbm, hbm],
        out_specs=(vmem,) * 6,
        scratch_shapes=[
            pltpu.VMEM((key_heads, pool, page, hd), BF16),
            pltpu.VMEM((key_heads, pool, page, hd), BF16),
            pltpu.VMEM((pool, req), F32),
            pltpu.VMEM((pool, nx), F32),
            pltpu.VMEM((key_heads, hd + 16, tokens), BF16),
            pltpu.VMEM((2, tokens, 256), F32),
            pltpu.VMEM((key_heads, nx, hd), BF16),
            pltpu.VMEM((ni, padded, hd), F32),
            slots,
            slots,
            slots,
            slots,
            pltpu.VMEM((8, 128), F32),
            pltpu.VMEM((8, req), F32),
            pltpu.VMEM((ni, 8, 128), F32),
            pltpu.VMEM((nt, 8, req), F32),
            pltpu.VMEM((8, nx), F32),
            pltpu.VMEM((ni, 8, nx), F32),
            pltpu.SemaphoreType.DMA((2, key_heads)),
            pltpu.SemaphoreType.DMA((2, ni)),
            pltpu.SemaphoreType.DMA((2, nt)),
            pltpu.SemaphoreType.DMA((2, ni)),
            pltpu.SemaphoreType.DMA((2, ni)),
            pltpu.SemaphoreType.DMA((2, ni)),
        ],
        compiler_params=params(collective_id=0, has_side_effects=True),
        cost_estimate=pl.CostEstimate(
            flops=4 * heads * (req + ni) * tokens * hd,
            bytes_accessed=4 * pool_keys.size,
            transcendentals=heads * req * tokens,
        ),
        name="attend",
    )(
        move_target.T, move_request[None, :], squares[None, :], move_target[:, 0], move_page, by_head, page_table.T, lengths[None, :],
        pool_keys, pool_values,
    )

    me = lax.axis_index("inst").astype(jnp.int32).reshape(1)
    attention_out, new_kv = pl.pallas_call(
        functools.partial(join_kernel, features, group, heads),
        out_shape=(
            jax.ShapeDtypeStruct((req, heads * hd), BF16),
            jax.ShapeDtypeStruct((req, key_heads * 2 * hd), BF16),
        ),
        in_specs=[smem] + [vmem] * 9,
        out_specs=(vmem,) * 2,
        compiler_params=params(),
        name="join",
    )(
        me, moved_in, levels_in, label, local, levels, by_head, projected, sq_total,
        lengths[None, :],
    )
    return (attention_out, new_kv.reshape(req, key_heads, 2 * hd))


def solution(mesh):
    return jax.shard_map(
        body,
        mesh=mesh,
        in_specs=(
            P("inst", "tp"),
            P("tp"),
            P("tp", None, None),
            P("inst", "tp", None),
            P("inst", "tp", None, None),
            P("inst", "tp", None, None),
            P("inst", None),
            P("inst"),
            P("inst", None),
            P("inst"),
            P("inst"),
        ),
        out_specs=(P("inst", "tp"), P("inst", "tp", None)),
        check_vma=False,
    )
```
